32 devices in a mesh: grp: 8 (over z, x), tp: 4 (over y, core).
Axes of the slice: x: 2, y: 2, z: 4, core: 2. Of those that a mesh axis runs over, the one named last changes fastest.
Arguments:
- features: bfloat16 [96, 128, 8192], P('grp', None, 'tp'), may hold values from -6 to 6
- tile_request: int32 [96], P('grp'), may hold values from 0 to 63, as said below
- tile_rows: int32 [96], P('grp'), may hold values from 0 to 128, as said below
- key_weight: bfloat16 [8192, 1024], P('tp'), may hold values from -0.0625 to 0.0625
- value_weight: bfloat16 [8192, 1024], P('tp'), may hold values from -0.0625 to 0.0625
- key_gain: float32 [128], replicated, may hold values from 0.1 to 1.9
- cached_keys: bfloat16 [64, 512, 1024], P('grp', None, 'tp'), may hold values from -3 to 3
- cached_values: bfloat16 [64, 512, 1024], P('grp', None, 'tp'), may hold values from -6 to 6
- cache_len: int32 [64], P('grp'), may hold values from 2 to 512, as said below
- queries: bfloat16 [2, 64, 8192], P(None, 'grp', 'tp'), may hold values from -8 to 8
Outputs:
- context: bfloat16 [2, 64, 8192], P(None, 'grp', 'tp')
The draws below stay inside these ranges and needn't reach their ends.
Inputs may be any that keep to these rules, and one draw needn't show every extreme that they name: `tile_request`: request r belongs to decode group r // 8. The 12 tiles of one encoder device (aligned blocks) hold at most 2 tiles for one decode group, and at most 16 tiles in all serve one group's requests; both bounds are reached in every draw. A group's tiles are spread evenly over its requests, so no request has more than 2 tiles, rounded up. `tile_rows`: A tile is either live in all 128 rows or a padding tile with 0 live rows. `cache_len`: cached positions at or past a request's count are unused.
All inputs are finite; a program needn't handle non-finite values.
Results may differ from the reference program's by a relative error of at most 0.0059.
Values may be sent and summed in bfloat16 or wider, within the bound.
A program may use at most 128 MiB of HBM per device.

```python
import jax
import jax.numpy as jnp
from jax import lax

FEAT = 8192
KVH = 8
NH = 64
HD = 128
REQ_DEV = 8
TILE_DEV = 12
ROWS = 128
CACHE = 512
STEPS = 2
REQUESTS = 64
TILES = 96
GCAP = 16
N_GRP = 8


def draw_tile_request(key, part):
    key = jax.random.fold_in(key, 3)
    subkeys = jax.random.split(key, 5)
    group_order = jax.random.permutation(subkeys[0], N_GRP)
    swings = jax.random.randint(subkeys[1], (N_GRP // 2,), 0, GCAP - TILE_DEV + 1)
    swings = swings.at[0].set(GCAP - TILE_DEV)
    signed = jnp.stack([swings, -swings], axis=1).reshape(N_GRP)
    group_loads = jnp.zeros((N_GRP,), jnp.int32).at[group_order].set(TILE_DEV + signed)
    group_ends = jnp.cumsum(group_loads)
    column = jax.random.permutation(subkeys[2], N_GRP)
    within = jax.vmap(lambda subkey: jax.random.permutation(subkey, TILE_DEV))(jax.random.split(subkeys[3], N_GRP))
    serial = within * N_GRP + column[:, None]
    target = jnp.sum((serial[:, :, None] >= group_ends[None, None, :]).astype(jnp.int32), axis=2)
    group_starts = group_ends - group_loads
    rank_in_group = serial - group_starts[target]
    slot_orders = jax.vmap(lambda subkey: jax.random.permutation(subkey, REQ_DEV))(jax.random.split(subkeys[4], N_GRP))
    local_slot = slot_orders[target, rank_in_group % REQ_DEV]
    return (target * REQ_DEV + local_slot).reshape(N_GRP * TILE_DEV).astype(jnp.int32)


def draw_tile_rows(key, part):
    key = jax.random.fold_in(key, 5)
    subkeys = jax.random.split(key, 3)
    live = jax.random.randint(subkeys[0], (TILES,), 0, 4) != 0
    counts = jnp.where(live, ROWS, 0)
    longest = jax.random.randint(subkeys[1], (), 0, TILES)
    shortest = (longest + 1 + jax.random.randint(subkeys[2], (), 0, TILES - 1)) % TILES
    counts = counts.at[longest].set(ROWS).at[shortest].set(0)
    return counts.astype(jnp.int32)


def draw_cache_len(key, part):
    key = jax.random.fold_in(key, 7)
    subkeys = jax.random.split(key, 3)
    counts = jax.random.randint(subkeys[0], (REQUESTS,), 2, CACHE + 1)
    longest = jax.random.randint(subkeys[1], (), 0, REQUESTS)
    shortest = (longest + 1 + jax.random.randint(subkeys[2], (), 0, REQUESTS - 1)) % REQUESTS
    counts = counts.at[longest].set(CACHE).at[shortest].set(2)
    return counts.astype(jnp.int32)


def draw_cached_keys(key, part):
    key = jax.random.fold_in(key, 11)
    values = jnp.clip(jax.random.normal(key, (REQUESTS, CACHE, KVH, HD), jnp.float32), -3.0, 3.0)
    return values.reshape(REQUESTS, CACHE, KVH * HD).astype(jnp.bfloat16)


def draw_queries(key, part):
    key = jax.random.fold_in(key, 13)
    values = jnp.clip(2.0 * jax.random.normal(key, (STEPS, REQUESTS, NH, HD), jnp.float32), -8.0, 8.0)
    return values.reshape(STEPS, REQUESTS, NH * HD).astype(jnp.bfloat16)


def level_of(rng, shape, cuts, least, top_value):
    level = 1.0
    for dim, blocks in cuts:
        steps = jax.random.uniform(jax.random.fold_in(jax.random.fold_in(rng, 6), dim), (blocks,), jnp.float32, least / len(cuts), top_value / len(cuts))
        level = level * jnp.repeat(jnp.exp(steps), shape[dim] // blocks).reshape((-1,) + (1,) * (len(shape) - 1 - dim))
    return level


def noise(own_key, shape, scale, bound, shards=(), kind=jnp.bfloat16):
    factor_of = level_of(own_key, shape, shards, -0.22, 0.18) if shards else 1.0
    values = jax.random.normal(own_key, shape, jnp.float32) * scale * factor_of
    return jnp.minimum(jnp.maximum(values, -bound), bound).astype(kind)


def setup_inputs(seed: int = 0) -> dict:
    keys = jax.random.split(jax.random.key(seed), 11)
    features = noise(keys[0], (TILES, ROWS, FEAT), 1.0, 6.0, ((0, 8), (2, 4)))
    tile_request = draw_tile_request(jax.random.fold_in(keys[10], 71), 0)
    tile_rows = draw_tile_rows(jax.random.fold_in(keys[10], 71), 0)
    key_weight = noise(keys[3], (FEAT, KVH * HD), FEAT ** -0.5, 0.0625, ((0, 4),))
    value_weight = noise(keys[4], (FEAT, KVH * HD), FEAT ** -0.5, 0.0625, ((0, 4),))
    key_gain = jnp.clip(1.0 + 0.18 * jax.random.normal(keys[5], (HD,), jnp.float32), 0.1, 1.9)
    cached_keys = draw_cached_keys(jax.random.fold_in(keys[10], 71), 0)
    cached_values = noise(keys[7], (REQUESTS, CACHE, KVH * HD), 1.0, 6.0, ((0, 8), (2, 4)))
    cache_len = draw_cache_len(jax.random.fold_in(keys[10], 71), 0)
    queries = draw_queries(jax.random.fold_in(keys[10], 71), 0)
    return {"features": features, "tile_request": tile_request, "tile_rows": tile_rows, "key_weight": key_weight, "value_weight": value_weight, "key_gain": key_gain, "cached_keys": cached_keys, "cached_values": cached_values, "cache_len": cache_len, "queries": queries}


EPSILON = 1e-05

def key_norm(raw_rows, gain):
    scale = lax.rsqrt(lax.optimization_barrier(jnp.mean(raw_rows * raw_rows, axis=-1, keepdims=True)) + EPSILON)
    return raw_rows * scale * gain

def attend(query_block, cache_keys, cache_values, cache_count, new_keys, new_values, new_request, new_count):
    factor = query_block.shape[-1] ** (-0.5)
    query_wide = query_block.astype(jnp.float32)
    cache_scores = jnp.einsum('srhgd,rchd->srhgc', query_wide, cache_keys.astype(jnp.float32)) * factor
    new_scores = jnp.einsum('srhgd,nthd->srhgnt', query_wide, new_keys.astype(jnp.float32)) * factor
    requests_here = query_block.shape[1]
    cache_mask = jnp.arange(cache_keys.shape[1])[None, :] < cache_count[:, None]
    cache_mask = cache_mask[None, :, None, None, :]
    row_live = jnp.arange(new_keys.shape[1])[None, :] < new_count[:, None]
    belongs = new_request[None, :] == jnp.arange(requests_here)[:, None]
    new_mask = (belongs[:, :, None] & row_live[None, :, :])[None, :, None, None, :, :]
    floor_value = -1e+30
    cache_masked = jnp.where(cache_mask, cache_scores, floor_value)
    new_masked = jnp.where(new_mask, new_scores, floor_value)
    row_peak = jnp.maximum(lax.optimization_barrier(jnp.max(cache_masked, axis=-1)), lax.optimization_barrier(jnp.max(new_masked, axis=(-2, -1))))
    cache_exp = jnp.where(cache_mask, jnp.exp(cache_masked - row_peak[..., None]), 0.0)
    new_exp = jnp.where(new_mask, jnp.exp(new_masked - row_peak[..., None, None]), 0.0)
    denominator = lax.optimization_barrier(jnp.sum(cache_exp, axis=-1)) + lax.optimization_barrier(jnp.sum(new_exp, axis=(-2, -1)))
    cache_weights = (cache_exp / denominator[..., None]).astype(jnp.bfloat16)
    new_weights = (new_exp / denominator[..., None, None]).astype(jnp.bfloat16)
    context = jnp.einsum('srhgc,rchd->srhgd', cache_weights.astype(jnp.float32), cache_values.astype(jnp.float32))
    context = context + jnp.einsum('srhgnt,nthd->srhgd', new_weights.astype(jnp.float32), new_values.astype(jnp.float32))
    return context.astype(jnp.bfloat16)

def reference(features, tile_request, tile_rows, key_weight, value_weight, key_gain, cached_keys, cached_values, cache_len, queries):
    tile_total = features.shape[0]
    flat_rows = features.reshape(tile_total * ROWS, FEAT)
    raw_keys = jnp.dot(flat_rows, key_weight, preferred_element_type=jnp.float32).reshape(tile_total, ROWS, KVH, HD)
    raw_values = jnp.dot(flat_rows, value_weight, preferred_element_type=jnp.float32).reshape(tile_total, ROWS, KVH, HD)
    new_keys = key_norm(raw_keys, key_gain).astype(jnp.bfloat16)
    new_values = raw_values.astype(jnp.bfloat16)
    group_size = NH // KVH

    def one_group(group_index):
        start = (group_index * REQ_DEV).astype(jnp.int32)
        is_live = tile_request // REQ_DEV == group_index
        position = jnp.cumsum(is_live.astype(jnp.int32)) - 1
        select = is_live[None, :] & (position[None, :] == jnp.arange(GCAP)[:, None])
        present = jnp.any(select, axis=1)
        source = lax.optimization_barrier(jnp.sum(jnp.where(select, jnp.arange(tile_total)[None, :], 0), axis=1)).astype(jnp.int32)
        request_here = jnp.where(present, tile_request[source] - start, -1).astype(jnp.int32)
        rows_here = jnp.where(present, tile_rows[source], 0).astype(jnp.int32)
        query_block = lax.dynamic_slice_in_dim(queries, start, REQ_DEV, 1).reshape(STEPS, REQ_DEV, KVH, group_size, HD)
        cache_block = lax.dynamic_slice_in_dim(cached_keys, start, REQ_DEV, 0).reshape(REQ_DEV, CACHE, KVH, HD)
        value_block = lax.dynamic_slice_in_dim(cached_values, start, REQ_DEV, 0).reshape(REQ_DEV, CACHE, KVH, HD)
        counts = lax.dynamic_slice_in_dim(cache_len, start, REQ_DEV, 0)
        context = attend(query_block, cache_block, value_block, counts, new_keys[source], new_values[source], request_here, rows_here)
        return context.reshape(STEPS, REQ_DEV, NH * HD)
    blocks = lax.map(one_group, jnp.arange(N_GRP, dtype=jnp.int32))
    return jnp.transpose(blocks, (1, 0, 2, 3)).reshape(STEPS, N_GRP * REQ_DEV, NH * HD)
```

```python
import jax
import jax.numpy as jnp
from jax import lax
from jax.sharding import PartitionSpec as P

KVH = 8
NH = 64
HD = 128
EPSILON = 1e-05
FLOOR = -1e30


def key_norm(raw_rows, gain):
    scale = lax.rsqrt(jnp.mean(raw_rows * raw_rows, axis=-1, keepdims=True) + EPSILON)
    return raw_rows * scale * gain


def split_attend(scores, mask, values, spec):
    masked = jnp.where(mask, scores, FLOOR)
    peak = jnp.max(masked, axis=-1, keepdims=True)
    weights = jnp.where(mask, jnp.exp(masked - peak), 0.0)
    total = jnp.sum(weights, axis=-1, keepdims=True)
    out = jnp.einsum(spec, weights.astype(jnp.bfloat16), values, preferred_element_type=jnp.float32)
    live = total > 0
    safe = jnp.where(live, total, 1.0)
    return out / safe, jnp.where(live, peak + jnp.log(safe), FLOOR)


def on_device(
    features, tile_request, tile_rows, key_weight, value_weight, key_gain,
    cached_keys, cached_values, cache_len, queries,
):
    groups = lax.axis_size("grp")
    tensor = lax.axis_size("tp")
    tiles, tile_len, feat_cols = features.shape
    heads = KVH // tensor
    per = NH // KVH
    steps = queries.shape[0]
    requests = cache_len.shape[0]
    cache_slots = cached_keys.shape[1]
    peer_slots = -(-tiles // groups)
    slot_total = groups * peer_slots
    me = lax.axis_index("grp")
    factor = HD ** (-0.5)

    all_q = lax.all_gather(queries, "grp", axis=0, tiled=False)
    all_req = lax.all_gather(tile_request, "grp", axis=0, tiled=False)
    flat = features.reshape(tiles * tile_len, feat_cols)
    part_keys = jnp.dot(flat, key_weight, preferred_element_type=jnp.float32)
    part_values = jnp.dot(flat, value_weight, preferred_element_type=jnp.float32)
    sum_keys = lax.psum_scatter(part_keys, "tp", scatter_dimension=1, tiled=True)
    sum_values = lax.psum_scatter(part_values, "tp", scatter_dimension=1, tiled=True)
    new_keys = key_norm(sum_keys.reshape(tiles, tile_len, heads, HD), key_gain).astype(jnp.bfloat16)
    new_values = sum_values.astype(jnp.bfloat16).reshape(tiles, tile_len, heads, HD)

    q_all = all_q.transpose(0, 2, 1, 3).reshape(groups * requests, steps, heads, per, HD)
    q_tile = q_all[tile_request]
    scores = jnp.einsum("nshgd,nthd->nhsgt", q_tile, new_keys, preferred_element_type=jnp.float32) * factor
    mask = (jnp.arange(tile_len)[None, :] < tile_rows[:, None])[:, None, None, None, :]
    tile_out, tile_lse = split_attend(scores, mask, new_values, "nhsgt,nthd->nhsgd")

    earlier = jnp.arange(tiles)[None, :] < jnp.arange(tiles)[:, None]
    target = tile_request // requests
    rank = jnp.sum((target[:, None] == target[None, :]) & earlier, axis=1)
    slot = target * peer_slots + rank
    select = slot[None, :] == jnp.arange(slot_total)[:, None]
    present = jnp.any(select, axis=1)
    source = jnp.sum(jnp.where(select, jnp.arange(tiles)[None, :], 0), axis=1)
    out_slots = tile_out[source]
    lse_slots = jnp.where(present[:, None, None, None, None], tile_lse[source], FLOOR)
    payload = jnp.concatenate([out_slots, lse_slots], axis=-1)
    got = lax.all_to_all(payload, "grp", split_axis=0, concat_axis=0, tiled=True)
    got_out, got_lse = got[..., :HD], got[..., HD:]

    all_target = all_req // requests
    all_rank = jnp.sum((all_target[:, :, None] == all_target[:, None, :]) & earlier[None], axis=2)
    hit = (all_target[:, None, :] == me) & (all_rank[:, None, :] == jnp.arange(peer_slots)[None, :, None])
    slot_req = jnp.where(jnp.any(hit, axis=2), jnp.sum(jnp.where(hit, all_req[:, None, :] - me * requests, 0), axis=2), -1)
    slot_req = slot_req.reshape(slot_total)

    q_block = queries.reshape(steps, requests, heads, per, HD)
    c_keys = cached_keys.reshape(requests, cache_slots, heads, HD)
    c_values = cached_values.reshape(requests, cache_slots, heads, HD)
    c_scores = jnp.einsum("srhgd,rchd->rhsgc", q_block, c_keys, preferred_element_type=jnp.float32) * factor
    c_mask = (jnp.arange(cache_slots)[None, :] < cache_len[:, None])[:, None, None, None, :]
    c_out, c_lse = split_attend(c_scores, c_mask, c_values, "rhsgc,rchd->rhsgd")

    belongs = (slot_req[None, :] == jnp.arange(requests)[:, None])[:, :, None, None, None, None]
    r_lse = jnp.where(belongs, got_lse[None], FLOOR)
    peak = jnp.maximum(c_lse, jnp.max(r_lse, axis=1))
    c_w = jnp.exp(c_lse - peak)
    r_w = jnp.where(belongs, jnp.exp(r_lse - peak[:, None]), 0.0)
    num = c_w * c_out + jnp.sum(jnp.where(belongs, r_w * got_out[None], 0.0), axis=1)
    den = c_w + jnp.sum(r_w, axis=1)
    context = (num / den).astype(jnp.bfloat16)
    return context.transpose(2, 0, 1, 3, 4).reshape(steps, requests, heads * per * HD)


def solution(mesh):
    in_specs = (
        P("grp", None, "tp"), P("grp"), P("grp"), P("tp", None), P("tp", None), P(),
        P("grp", None, "tp"), P("grp", None, "tp"), P("grp"), P(None, "grp", "tp"),
    )
    return jax.shard_map(
        on_device, mesh=mesh, in_specs=in_specs, out_specs=P(None, "grp", "tp"), check_vma=False
    )
```

```python
import functools

import jax
import jax.numpy as jnp
from jax import lax
from jax.experimental import pallas as pl
from jax.experimental.pallas import tpu as pltpu
from jax.sharding import PartitionSpec as P

KVH = 8
NH = 64
HD = 128
EPSILON = 1e-05
FLOOR = -1e30
CORES = 2
CORE_TYPE = jnp.float32
MESH = pl.DeviceIdType.MESH


def attend(query, keys, values, live_count):
    scores = lax.dot_general(
        query, keys, (((1,), (1,)), ((), ())), preferred_element_type=jnp.float32
    ) * (HD ** -0.5)
    live = lax.broadcasted_iota(jnp.int32, scores.shape, 1) < live_count
    scores = jnp.where(live, scores, FLOOR)
    peak = jnp.max(scores, axis=1, keepdims=True)
    weights = jnp.where(live, jnp.exp(scores - peak), 0.0)
    total = jnp.sum(weights, axis=1, keepdims=True)
    out = jnp.dot(weights.astype(jnp.bfloat16), values, preferred_element_type=jnp.float32)
    some = total > 0
    safe = jnp.where(some, total, 1.0)
    return out / safe, jnp.where(some, peak + jnp.log(safe), FLOOR)


def kernel(
    groups, tensor, tiles, tile_len, requests, chunks,
    req_ref, rows_ref, len_ref, gain_ref, q_ref, feat_ref, kw_ref, vw_ref, ck_ref, cv_ref,
    out_ref,
    fbuf, wbuf, ckbuf, cvbuf, allq, csend, crecv, own, keep, ysend, yrecv,
    cache_out, cache_lse, tile_out, tile_lse, send_out, send_lse, got_out, got_lse, slot_lse, slot_req,
    fsem, wsem, csem, qsend, qrecv, cs_sem, cr_sem, ys_sem, yr_sem, os_sem, or_sem, ls_sem, lr_sem,
):
    ys = tensor // CORES
    heads = KVH // tensor
    width = heads * HD
    chunk = tiles * tile_len // chunks
    per_chunk = tiles // chunks
    peer_slots = -(-tiles // groups)
    qrows = q_ref.shape[2]
    me = lax.axis_index("grp")
    tp = lax.axis_index("tp")
    y, core = tp // CORES, tp % CORES
    partner = y * CORES + (1 - core)

    def y_peer(k):
        return lax.rem(y + k, ys) * CORES + core

    def grp_peer(k):
        return lax.rem(me + k, groups)

    def feat_copy(i):
        return pltpu.make_async_copy(
            feat_ref.at[pl.ds(pl.multiple_of(i * chunk, chunk), chunk)], fbuf.at[i], fsem.at[i]
        )

    def weight_copy(side, k, kv):
        col_core = (1 - core) if side == 0 else core
        col = pl.multiple_of((lax.rem(y + k, ys) * CORES + col_core) * width, width)
        return pltpu.make_async_copy(
            (kw_ref, vw_ref)[kv].at[:, pl.ds(col, width)], wbuf.at[side, k, kv], wsem.at[side, k, kv]
        )

    order = [k % ys for k in range(1, ys + 1)]
    feat_copy(0).start()
    for side in range(2):
        for k in order:
            for kv in range(2):
                weight_copy(side, k, kv).start()
        if side == 0:
            for i in range(1, chunks):
                feat_copy(i).start()
    key_copy = pltpu.make_async_copy(ck_ref, ckbuf, csem.at[0])
    value_copy = pltpu.make_async_copy(cv_ref, cvbuf, csem.at[1])
    key_copy.start()
    value_copy.start()

    barrier = pltpu.get_barrier_semaphore()
    pl.semaphore_signal(barrier, inc=1, device_id={"tp": partner}, device_id_type=MESH)
    for k in range(1, ys):
        pl.semaphore_signal(barrier, inc=1, device_id={"tp": y_peer(k)}, device_id_type=MESH)
    for k in range(1, groups):
        pl.semaphore_signal(barrier, inc=1, device_id={"grp": grp_peer(k)}, device_id_type=MESH)
    pl.semaphore_wait(barrier, 1 + (ys - 1) + (groups - 1))

    allq[pl.ds(pl.multiple_of(me * requests, requests), requests)] = q_ref[...]

    def query_copy(k):
        return pltpu.make_async_remote_copy(
            src_ref=q_ref,
            dst_ref=allq.at[pl.ds(pl.multiple_of(me * requests, requests), requests)],
            send_sem=qsend.at[k], recv_sem=qrecv.at[k],
            device_id={"grp": grp_peer(k)}, device_id_type=MESH,
        )

    for k in range(1, groups):
        query_copy(k).start()

    def core_copy(i):
        return pltpu.make_async_remote_copy(
            src_ref=csend.at[i], dst_ref=crecv.at[i],
            send_sem=cs_sem.at[i], recv_sem=cr_sem.at[i],
            device_id={"tp": partner}, device_id_type=MESH,
        )

    def y_copy(i, k):
        return pltpu.make_async_remote_copy(
            src_ref=ysend.at[i, k - 1], dst_ref=yrecv.at[i, k - 1],
            send_sem=ys_sem.at[i, k - 1], recv_sem=yr_sem.at[i, k - 1],
            device_id={"tp": y_peer(k)}, device_id_type=MESH,
        )

    def give(i, wait):
        for k in order:
            for kv in range(2):
                if wait:
                    weight_copy(0, k, kv).wait()
                csend[i, k, kv] = jnp.dot(
                    fbuf[i], wbuf[0, k, kv], preferred_element_type=jnp.float32
                ).astype(csend.dtype)
        core_copy(i).start()

    feat_copy(0).wait()
    give(0, True)
    for k in order:
        for kv in range(2):
            weight_copy(1, k, kv).wait()

    def step(i, carry):
        for k in order:
            for kv in range(2):
                own[k, kv] = jnp.dot(fbuf[i], wbuf[1, k, kv], preferred_element_type=jnp.float32)

        @pl.when(i + 1 < chunks)
        def _():
            feat_copy(i + 1).wait()
            give(i + 1, False)

        core_copy(i).wait_recv()
        for k in range(1, ys):
            ysend[i, k - 1] = (own[k] + crecv[i, k].astype(jnp.float32)).astype(jnp.bfloat16)
            y_copy(i, k).start()
        keep[i] = own[0] + crecv[i, 0].astype(jnp.float32)
        return carry

    lax.fori_loop(0, chunks, step, 0)

    key_copy.wait()
    value_copy.wait()

    def cached(r, carry):
        for h in range(heads):
            cols = pl.ds(h * HD, HD)
            o, lse = attend(q_ref[r, h], ckbuf[r, :, cols], cvbuf[r, :, cols], len_ref[r])
            cache_out[r, h] = o
            cache_lse[r, h] = jnp.broadcast_to(lse, (qrows, HD))
        return carry

    lax.fori_loop(0, requests, cached, 0)
    for k in range(1, groups):
        query_copy(k).wait()

    gain = gain_ref[...]

    def fresh(i, carry):
        for k in range(1, ys):
            y_copy(i, k).wait_recv()
        for u in range(per_chunk):
            t = i * per_chunk + u
            rows = pl.ds(u * tile_len, tile_len)
            for h in range(heads):
                cols = pl.ds(h * HD, HD)
                raw_k = keep[i, 0, rows, cols]
                raw_v = keep[i, 1, rows, cols]
                for k in range(1, ys):
                    raw_k = raw_k + yrecv[i, k - 1, 0, rows, cols].astype(jnp.float32)
                    raw_v = raw_v + yrecv[i, k - 1, 1, rows, cols].astype(jnp.float32)
                scale = lax.rsqrt(jnp.mean(raw_k * raw_k, axis=1, keepdims=True) + EPSILON)
                new_k = (raw_k * scale * gain).astype(jnp.bfloat16)
                o, lse = attend(allq[req_ref[t], h], new_k, raw_v.astype(jnp.bfloat16), rows_ref[t])
                tile_out[t, h] = o.astype(jnp.bfloat16)
                tile_lse[t, h] = jnp.broadcast_to(lse, (qrows, HD))
        return carry

    lax.fori_loop(0, chunks, fresh, 0)

    reqs = [req_ref[t] for t in range(tiles)]
    targets = [r // requests for r in reqs]
    ranks = []
    for t in range(tiles):
        rank = jnp.int32(0)
        for s in range(t):
            rank = rank + (targets[s] == targets[t]).astype(jnp.int32)
        ranks.append(rank)
    lane = lax.broadcasted_iota(jnp.int32, (heads, qrows, HD), 2)

    def out_copy(k):
        return pltpu.make_async_remote_copy(
            src_ref=send_out.at[k], dst_ref=got_out.at[k],
            send_sem=os_sem.at[k], recv_sem=or_sem.at[k],
            device_id={"grp": grp_peer(k)}, device_id_type=MESH,
        )

    def lse_copy(k):
        return pltpu.make_async_remote_copy(
            src_ref=send_lse.at[k], dst_ref=got_lse.at[k],
            send_sem=ls_sem.at[k], recv_sem=lr_sem.at[k],
            device_id={"grp": grp_peer(k)}, device_id_type=MESH,
        )

    for k in list(range(1, groups)) + [0]:
        group = grp_peer(k)
        packed = jnp.full((heads, qrows, HD), FLOOR, jnp.float32)
        o_to, l_to = (send_out, send_lse) if k else (got_out, got_lse)
        for j in range(peer_slots):
            source = jnp.int32(0)
            found = jnp.int32(0)
            for t in range(tiles):
                here = ((targets[t] == group) & (ranks[t] == j)).astype(jnp.int32)
                source = source + here * t
                found = found + here
            o_to[k, j] = tile_out[source]
            local = jnp.where(found > 0, req_ref[source] - group * requests, -1)
            lse = jnp.where(found > 0, tile_lse[source], FLOOR)
            packed = jnp.where(lane == j, lse, packed)
            packed = jnp.where(lane == HD // 2 + j, local.astype(jnp.float32), packed)
        l_to[k] = packed
        if k:
            lse_copy(k).start()
            out_copy(k).start()

    for i in range(chunks):
        core_copy(i).wait_send()
        for k in range(1, ys):
            y_copy(i, k).wait_send()
    for k in range(1, groups):
        lse_copy(k).wait()
        out_copy(k).wait()

    for k in range(groups):
        for j in range(peer_slots):
            s = k * peer_slots + j
            slot_lse[s] = jnp.broadcast_to(got_lse[k, :, :, j : j + 1], (heads, qrows, HD))
            slot_req[s] = jnp.broadcast_to(
                got_lse[k, :, :, HD // 2 + j : HD // 2 + j + 1], (heads, qrows, HD)
            )

    def merge(r, carry):
        want = r.astype(jnp.float32)
        base = cache_lse[r]
        peak = base
        for s in range(groups * peer_slots):
            peak = jnp.maximum(peak, jnp.where(slot_req[s] == want, slot_lse[s], FLOOR))
        weight = jnp.exp(base - peak)
        num = weight * cache_out[r]
        den = weight
        for k in range(groups):
            for j in range(peer_slots):
                s = k * peer_slots + j
                mine = slot_req[s] == want
                weight = jnp.where(mine, jnp.exp(jnp.where(mine, slot_lse[s], FLOOR) - peak), 0.0)
                num = num + weight * got_out[k, j].astype(jnp.float32)
                den = den + weight
        out_ref[r] = (num / den).astype(jnp.bfloat16)
        return carry

    lax.fori_loop(0, requests, merge, 0)


def on_device(
    features, tile_request, tile_rows, key_weight, value_weight, key_gain,
    cached_keys, cached_values, cache_len, queries,
):
    groups = lax.axis_size("grp")
    tensor = lax.axis_size("tp")
    tiles, tile_len, feat = features.shape
    ys = tensor // CORES
    heads = KVH // tensor
    width = heads * HD
    per = NH // KVH
    steps = queries.shape[0]
    requests = cache_len.shape[0]
    cache_slots = cached_keys.shape[1]
    peer_slots = -(-tiles // groups)
    qrows = steps * per
    chunks = 6 if tiles % 6 == 0 else tiles
    chunk = tiles * tile_len // chunks
    hops = max(ys - 1, 1)
    q = queries.reshape(steps, requests, heads, per, HD).transpose(1, 2, 0, 3, 4)
    q = q.reshape(requests, heads, qrows, HD)
    bf, f32 = jnp.bfloat16, jnp.float32
    vmem = pl.BlockSpec(memory_space=pltpu.VMEM)
    smem = pl.BlockSpec(memory_space=pltpu.SMEM)
    hbm = pl.BlockSpec(memory_space=pl.ANY)
    dma = pltpu.SemaphoreType.DMA
    slots = groups * peer_slots
    out = pl.pallas_call(
        functools.partial(kernel, groups, tensor, tiles, tile_len, requests, chunks),
        out_shape=jax.ShapeDtypeStruct((requests, heads, qrows, HD), bf),
        in_specs=[smem, smem, smem, vmem, vmem, hbm, hbm, hbm, hbm, hbm],
        out_specs=vmem,
        scratch_shapes=[
            pltpu.VMEM((chunks, chunk, feat), bf),
            pltpu.VMEM((2, ys, 2, feat, width), bf),
            pltpu.VMEM((requests, cache_slots, width), bf),
            pltpu.VMEM((requests, cache_slots, width), bf),
            pltpu.VMEM((groups * requests, heads, qrows, HD), bf),
            pltpu.VMEM((chunks, ys, 2, chunk, width), CORE_TYPE),
            pltpu.VMEM((chunks, ys, 2, chunk, width), CORE_TYPE),
            pltpu.VMEM((ys, 2, chunk, width), f32),
            pltpu.VMEM((chunks, 2, chunk, width), f32),
            pltpu.VMEM((chunks, hops, 2, chunk, width), bf),
            pltpu.VMEM((chunks, hops, 2, chunk, width), bf),
            pltpu.VMEM((requests, heads, qrows, HD), f32),
            pltpu.VMEM((requests, heads, qrows, HD), f32),
            pltpu.VMEM((tiles, heads, qrows, HD), bf),
            pltpu.VMEM((tiles, heads, qrows, HD), f32),
            pltpu.VMEM((groups, peer_slots, heads, qrows, HD), bf),
            pltpu.VMEM((groups, heads, qrows, HD), f32),
            pltpu.VMEM((groups, peer_slots, heads, qrows, HD), bf),
            pltpu.VMEM((groups, heads, qrows, HD), f32),
            pltpu.VMEM((slots, heads, qrows, HD), f32),
            pltpu.VMEM((slots, heads, qrows, HD), f32),
            dma((chunks,)), dma((2, ys, 2)), dma((2,)),
            dma((groups,)), dma((groups,)),
            dma((chunks,)), dma((chunks,)),
            dma((chunks, hops)), dma((chunks, hops)),
            dma((groups,)), dma((groups,)), dma((groups,)), dma((groups,)),
        ],
        compiler_params=pltpu.CompilerParams(
            collective_id=0, has_side_effects=True, vmem_limit_bytes=60 * 1024 * 1024
        ),
    )(
        tile_request, tile_rows, cache_len, key_gain.reshape(1, HD), q,
        features.reshape(tiles * tile_len, feat), key_weight, value_weight, cached_keys, cached_values,
    )
    out = out.reshape(requests, heads, steps, per, HD).transpose(2, 0, 1, 3, 4)
    return out.reshape(steps, requests, heads * per * HD)


def solution(mesh):
    in_specs = (
        P("grp", None, "tp"), P("grp"), P("grp"), P("tp", None), P("tp", None), P(),
        P("grp", None, "tp"), P("grp", None, "tp"), P("grp"), P(None, "grp", "tp"),
    )
    return jax.shard_map(
        on_device, mesh=mesh, in_specs=in_specs, out_specs=P(None, "grp", "tp"), check_vma=False
    )
```

```python
import functools

import jax
import jax.numpy as jnp
from jax import lax
from jax.experimental import pallas as pl
from jax.experimental.pallas import tpu as pltpu
from jax.sharding import PartitionSpec as P

KVH = 8
NH = 64
HD = 128
EPSILON = 1e-05
FLOOR = -1e30
CORES = 2
CORE_TYPE = jnp.float32
MESH = pl.DeviceIdType.MESH


def attend(query, keys, values, live_count):
    scores = lax.dot_general(
        query, keys, (((1,), (1,)), ((), ())), preferred_element_type=jnp.float32
    ) * (HD ** -0.5)
    live = lax.broadcasted_iota(jnp.int32, scores.shape, 1) < live_count
    scores = jnp.where(live, scores, FLOOR)
    peak = jnp.max(scores, axis=1, keepdims=True)
    weights = jnp.where(live, jnp.exp(scores - peak), 0.0)
    total = jnp.sum(weights, axis=1, keepdims=True)
    out = jnp.dot(weights.astype(jnp.bfloat16), values, preferred_element_type=jnp.float32)
    some = total > 0
    safe = jnp.where(some, total, 1.0)
    return out / safe, jnp.where(some, peak + jnp.log(safe), FLOOR)


def kernel(
    groups, tensor, tiles, tile_len, requests, chunks,
    req_ref, rows_ref, len_ref, gain_ref, qin_ref, feat_ref, kw_ref, vw_ref, ck_ref, cv_ref,
    out_ref,
    q_ref, fbuf, wbuf, ckbuf, cvbuf, allq, csend, crecv, own, keep, ysend, yrecv,
    cache_out, cache_lse, tile_out, tile_lse, send_out, send_lse, got_out, got_lse, slot_lse, slot_req,
    fsem, wsem, csem, qsend, qrecv, cs_sem, cr_sem, ys_sem, yr_sem, os_sem, or_sem, ls_sem, lr_sem,
):
    ys = tensor // CORES
    heads = KVH // tensor
    width = heads * HD
    chunk = tiles * tile_len // chunks
    per_chunk = tiles // chunks
    peer_slots = -(-tiles // groups)
    qrows = q_ref.shape[2]
    steps = qin_ref.shape[0]
    per = qrows // steps
    me = lax.axis_index("grp")
    tp = lax.axis_index("tp")
    y, core = tp // CORES, tp % CORES
    partner = y * CORES + (1 - core)

    def y_peer(k):
        return lax.rem(y + k, ys) * CORES + core

    def grp_peer(k):
        return lax.rem(me + k, groups)

    barrier = pltpu.get_barrier_semaphore()
    pl.semaphore_signal(barrier, inc=1, device_id={"tp": partner}, device_id_type=MESH)
    for k in range(1, ys):
        pl.semaphore_signal(barrier, inc=1, device_id={"tp": y_peer(k)}, device_id_type=MESH)
    for k in range(1, groups):
        pl.semaphore_signal(barrier, inc=1, device_id={"grp": grp_peer(k)}, device_id_type=MESH)

    def feat_copy(i):
        return pltpu.make_async_copy(
            feat_ref.at[pl.ds(pl.multiple_of(i * chunk, chunk), chunk)], fbuf.at[i], fsem.at[i]
        )

    def weight_copy(side, k, kv):
        col_core = (1 - core) if side == 0 else core
        col = pl.multiple_of((lax.rem(y + k, ys) * CORES + col_core) * width, width)
        return pltpu.make_async_copy(
            (kw_ref, vw_ref)[kv].at[:, pl.ds(col, width)], wbuf.at[side, k, kv], wsem.at[side, k, kv]
        )

    order = [k % ys for k in range(1, ys + 1)]
    feat_copy(0).start()
    for side in range(2):
        for k in order:
            for kv in range(2):
                weight_copy(side, k, kv).start()
        if side == 0:
            for i in range(1, chunks):
                feat_copy(i).start()
    key_copy = pltpu.make_async_copy(ck_ref, ckbuf, csem.at[0])
    value_copy = pltpu.make_async_copy(cv_ref, cvbuf, csem.at[1])
    key_copy.start()
    value_copy.start()

    total_rows = requests * qrows
    to = lax.broadcasted_iota(jnp.int32, (total_rows, total_rows), 0)
    frm = lax.broadcasted_iota(jnp.int32, (total_rows, total_rows), 1)
    swap = (lax.div(to, qrows) == lax.rem(frm, requests)) & (lax.rem(to, qrows) == lax.div(frm, requests))
    swap = jnp.where(swap, 1.0, 0.0).astype(jnp.bfloat16)
    for h in range(heads):
        rows = [
            qin_ref[s, :, pl.ds((h * per + g) * HD, HD)].astype(jnp.float32)
            for s in range(steps) for g in range(per)
        ]
        rows = jnp.concatenate(rows, axis=0).astype(jnp.bfloat16)
        rows = jnp.dot(swap, rows, preferred_element_type=jnp.float32).astype(jnp.bfloat16)
        for q in range(requests):
            q_ref[q, h] = rows[q * qrows : (q + 1) * qrows]
    allq[pl.ds(pl.multiple_of(me * requests, requests), requests)] = q_ref[...]

    def query_copy(k):
        return pltpu.make_async_remote_copy(
            src_ref=q_ref,
            dst_ref=allq.at[pl.ds(pl.multiple_of(me * requests, requests), requests)],
            send_sem=qsend.at[k], recv_sem=qrecv.at[k],
            device_id={"grp": grp_peer(k)}, device_id_type=MESH,
        )


    def core_copy(i):
        return pltpu.make_async_remote_copy(
            src_ref=csend.at[i], dst_ref=crecv.at[i],
            send_sem=cs_sem.at[i], recv_sem=cr_sem.at[i],
            device_id={"tp": partner}, device_id_type=MESH,
        )

    def y_copy(i, k):
        return pltpu.make_async_remote_copy(
            src_ref=ysend.at[i, k - 1], dst_ref=yrecv.at[i, k - 1],
            send_sem=ys_sem.at[i, k - 1], recv_sem=yr_sem.at[i, k - 1],
            device_id={"tp": y_peer(k)}, device_id_type=MESH,
        )

    def give(i, wait):
        for k in order:
            for kv in range(2):
                if wait:
                    weight_copy(0, k, kv).wait()
                csend[i, k, kv] = jnp.dot(
                    fbuf[i], wbuf[0, k, kv], preferred_element_type=jnp.float32
                ).astype(csend.dtype)
        if wait:
            pl.semaphore_wait(barrier, 1 + (ys - 1) + (groups - 1))
        core_copy(i).start()

    feat_copy(0).wait()
    give(0, True)
    for k in range(1, groups):
        query_copy(k).start()
    for k in order:
        for kv in range(2):
            weight_copy(1, k, kv).wait()

    def step(i, carry):
        for k in order:
            for kv in range(2):
                own[k, kv] = jnp.dot(fbuf[i], wbuf[1, k, kv], preferred_element_type=jnp.float32)

        @pl.when(i + 1 < chunks)
        def _():
            feat_copy(i + 1).wait()
            give(i + 1, False)

        core_copy(i).wait_recv()
        for k in range(1, ys):
            ysend[i, k - 1] = (own[k] + crecv[i, k].astype(jnp.float32)).astype(jnp.bfloat16)
            y_copy(i, k).start()
        keep[i] = own[0] + crecv[i, 0].astype(jnp.float32)
        return carry

    lax.fori_loop(0, chunks, step, 0)

    key_copy.wait()
    value_copy.wait()

    def cached(r, carry):
        for h in range(heads):
            cols = pl.ds(h * HD, HD)
            o, lse = attend(q_ref[r, h], ckbuf[r, :, cols], cvbuf[r, :, cols], len_ref[r])
            cache_out[r, h] = o
            cache_lse[r, h] = jnp.broadcast_to(lse, (qrows, HD))
        return carry

    lax.fori_loop(0, requests, cached, 0)
    for k in range(1, groups):
        query_copy(k).wait()

    gain = gain_ref[...]

    def fresh(i, carry):
        for k in range(1, ys):
            y_copy(i, k).wait_recv()
        for u in range(per_chunk):
            t = i * per_chunk + u
            rows = pl.ds(u * tile_len, tile_len)
            for h in range(heads):
                cols = pl.ds(h * HD, HD)
                raw_k = keep[i, 0, rows, cols]
                raw_v = keep[i, 1, rows, cols]
                for k in range(1, ys):
                    raw_k = raw_k + yrecv[i, k - 1, 0, rows, cols].astype(jnp.float32)
                    raw_v = raw_v + yrecv[i, k - 1, 1, rows, cols].astype(jnp.float32)
                scale = lax.rsqrt(jnp.mean(raw_k * raw_k, axis=1, keepdims=True) + EPSILON)
                new_k = (raw_k * scale * gain).astype(jnp.bfloat16)
                o, lse = attend(allq[req_ref[t], h], new_k, raw_v.astype(jnp.bfloat16), rows_ref[t])
                tile_out[t, h] = o.astype(jnp.bfloat16)
                tile_lse[t, h] = jnp.broadcast_to(lse, (qrows, HD))
        return carry

    lax.fori_loop(0, chunks, fresh, 0)

    reqs = [req_ref[t] for t in range(tiles)]
    targets = [r // requests for r in reqs]
    ranks = []
    for t in range(tiles):
        rank = jnp.int32(0)
        for s in range(t):
            rank = rank + (targets[s] == targets[t]).astype(jnp.int32)
        ranks.append(rank)
    lanes = send_lse.shape[1]
    lane = lax.broadcasted_iota(jnp.int32, (heads, qrows, HD), 2)

    def out_copy(k):
        return pltpu.make_async_remote_copy(
            src_ref=send_out.at[k], dst_ref=got_out.at[k],
            send_sem=os_sem.at[k], recv_sem=or_sem.at[k],
            device_id={"grp": grp_peer(k)}, device_id_type=MESH,
        )

    def lse_copy(k):
        return pltpu.make_async_remote_copy(
            src_ref=send_lse.at[k], dst_ref=got_lse.at[k],
            send_sem=ls_sem.at[k], recv_sem=lr_sem.at[k],
            device_id={"grp": grp_peer(k)}, device_id_type=MESH,
        )

    for k in list(range(1, groups)) + [0]:
        group = grp_peer(k)
        packed = jnp.full((heads, qrows, HD), FLOOR, jnp.float32)
        o_to, l_to = (send_out, send_lse) if k else (got_out, got_lse)
        for j in range(peer_slots):
            source = jnp.int32(0)
            found = jnp.int32(0)
            for t in range(tiles):
                here = ((targets[t] == group) & (ranks[t] == j)).astype(jnp.int32)
                source = source + here * t
                found = found + here
            o_to[k, j] = tile_out[source]
            local = jnp.where(found > 0, req_ref[source] - group * requests, -1)
            lse = jnp.where(found > 0, tile_lse[source], FLOOR)
            packed = jnp.where(lane == j, lse, packed)
            packed = jnp.where(lane == peer_slots + j, local.astype(jnp.float32), packed)
        l_to[k] = jnp.transpose(packed.reshape(heads * qrows, HD))[:lanes, :]
        if k:
            lse_copy(k).start()
            out_copy(k).start()

    for i in range(chunks):
        core_copy(i).wait_send()
        for k in range(1, ys):
            y_copy(i, k).wait_send()
    for k in range(1, groups):
        lse_copy(k).wait()
        out_copy(k).wait()

    for k in range(groups):
        flat = jnp.transpose(got_lse[k])
        for j in range(peer_slots):
            s = k * peer_slots + j
            lse = jnp.broadcast_to(flat[:, j : j + 1], (heads * qrows, HD))
            local = jnp.broadcast_to(flat[:, peer_slots + j : peer_slots + j + 1], (heads * qrows, HD))
            slot_lse[s] = lse.reshape(heads, qrows, HD)
            slot_req[s] = local.reshape(heads, qrows, HD)

    def merge(r, carry):
        want = r.astype(jnp.float32)
        base = cache_lse[r]
        peak = base
        for s in range(groups * peer_slots):
            peak = jnp.maximum(peak, jnp.where(slot_req[s] == want, slot_lse[s], FLOOR))
        weight = jnp.exp(base - peak)
        num = weight * cache_out[r]
        den = weight
        for k in range(groups):
            for j in range(peer_slots):
                s = k * peer_slots + j
                mine = slot_req[s] == want
                weight = jnp.where(mine, jnp.exp(jnp.where(mine, slot_lse[s], FLOOR) - peak), 0.0)
                num = num + weight * got_out[k, j].astype(jnp.float32)
                den = den + weight
        out_ref[r] = (num / den).astype(jnp.bfloat16)
        return carry

    lax.fori_loop(0, requests, merge, 0)


def on_device(
    features, tile_request, tile_rows, key_weight, value_weight, key_gain,
    cached_keys, cached_values, cache_len, queries,
):
    groups = lax.axis_size("grp")
    tensor = lax.axis_size("tp")
    tiles, tile_len, feat = features.shape
    ys = tensor // CORES
    heads = KVH // tensor
    width = heads * HD
    per = NH // KVH
    steps = queries.shape[0]
    requests = cache_len.shape[0]
    cache_slots = cached_keys.shape[1]
    peer_slots = -(-tiles // groups)
    qrows = steps * per
    chunks = tiles
    chunk = tiles * tile_len // chunks
    hops = max(ys - 1, 1)
    bf, f32 = jnp.bfloat16, jnp.float32
    vmem = pl.BlockSpec(memory_space=pltpu.VMEM)
    smem = pl.BlockSpec(memory_space=pltpu.SMEM)
    hbm = pl.BlockSpec(memory_space=pl.ANY)
    dma = pltpu.SemaphoreType.DMA
    slots = groups * peer_slots
    lanes = -(-2 * peer_slots // 8) * 8
    out = pl.pallas_call(
        functools.partial(kernel, groups, tensor, tiles, tile_len, requests, chunks),
        out_shape=jax.ShapeDtypeStruct((requests, heads, qrows, HD), bf),
        in_specs=[smem, smem, smem, vmem, vmem, hbm, hbm, hbm, hbm, hbm],
        out_specs=vmem,
        scratch_shapes=[
            pltpu.VMEM((requests, heads, qrows, HD), bf),
            pltpu.VMEM((chunks, chunk, feat), bf),
            pltpu.VMEM((2, ys, 2, feat, width), bf),
            pltpu.VMEM((requests, cache_slots, width), bf),
            pltpu.VMEM((requests, cache_slots, width), bf),
            pltpu.VMEM((groups * requests, heads, qrows, HD), bf),
            pltpu.VMEM((chunks, ys, 2, chunk, width), CORE_TYPE),
            pltpu.VMEM((chunks, ys, 2, chunk, width), CORE_TYPE),
            pltpu.VMEM((ys, 2, chunk, width), f32),
            pltpu.VMEM((chunks, 2, chunk, width), f32),
            pltpu.VMEM((chunks, hops, 2, chunk, width), bf),
            pltpu.VMEM((chunks, hops, 2, chunk, width), bf),
            pltpu.VMEM((requests, heads, qrows, HD), f32),
            pltpu.VMEM((requests, heads, qrows, HD), f32),
            pltpu.VMEM((tiles, heads, qrows, HD), bf),
            pltpu.VMEM((tiles, heads, qrows, HD), f32),
            pltpu.VMEM((groups, peer_slots, heads, qrows, HD), bf),
            pltpu.VMEM((groups, lanes, heads * qrows), f32),
            pltpu.VMEM((groups, peer_slots, heads, qrows, HD), bf),
            pltpu.VMEM((groups, lanes, heads * qrows), f32),
            pltpu.VMEM((slots, heads, qrows, HD), f32),
            pltpu.VMEM((slots, heads, qrows, HD), f32),
            dma((chunks,)), dma((2, ys, 2)), dma((2,)),
            dma((groups,)), dma((groups,)),
            dma((chunks,)), dma((chunks,)),
            dma((chunks, hops)), dma((chunks, hops)),
            dma((groups,)), dma((groups,)), dma((groups,)), dma((groups,)),
        ],
        compiler_params=pltpu.CompilerParams(
            collective_id=0, has_side_effects=True, vmem_limit_bytes=60 * 1024 * 1024
        ),
    )(
        tile_request, tile_rows, cache_len, key_gain.reshape(1, HD), queries,
        features.reshape(tiles * tile_len, feat), key_weight, value_weight, cached_keys, cached_values,
    )
    out = out.reshape(requests, heads, steps, per, HD).transpose(2, 0, 1, 3, 4)
    return out.reshape(steps, requests, heads * per * HD)


def solution(mesh):
    in_specs = (
        P("grp", None, "tp"), P("grp"), P("grp"), P("tp", None), P("tp", None), P(),
        P("grp", None, "tp"), P("grp", None, "tp"), P("grp"), P(None, "grp", "tp"),
    )
    return jax.shard_map(
        on_device, mesh=mesh, in_specs=in_specs, out_specs=P(None, "grp", "tp"), check_vma=False
    )
```
